32 devices in a mesh: tm: 4 (over y, x), pts: 8 (over z, core).
Axes of the slice: x: 2, y: 2, z: 4, core: 2. Of those that a mesh axis runs over, the one named last changes fastest.
Arguments:
- series: bfloat16 [8192, 3, 8192], P('tm', None, 'pts'), may hold values from -6 to 6
- weights: float32 [8192], P('pts'), may hold values from 1.2207031e-05 to 0.00012207031
- freq_bins: int32 [16], replicated, may hold values from 1 to 255
Outputs:
- cross_gram: float32 [16, 2, 32, 32], P('tm')
- spatial_modes: bfloat16 [16, 2, 32, 3, 8192], P('tm', None, None, None, 'pts')
The draws below stay inside these ranges and needn't reach their ends.
All inputs are finite; a program needn't handle non-finite values.
Results may differ from the reference program's by a relative error of at most 0.0067.
Values may be sent and summed in bfloat16 or wider, within the bound.
A program may use at most 128 MiB of HBM per device.

```python
import math
import jax
import jax.numpy as jnp
from jax import lax

NFFT = 512
NB = 32
NF = 16
ITERS = 4
PT_DEV = 1024
SAMPLES = 8192
PTS = 8192


def draw_series(key, part):
    region_count = PTS // PT_DEV
    noise_key = jax.random.fold_in(key, 11)
    signal_key = jax.random.fold_in(key, 23)
    loading_key = jax.random.fold_in(key, 37)
    amp_key = jax.random.fold_in(key, 41)
    point_region = jnp.arange(PTS, dtype=jnp.int32) // PT_DEV
    region_pos = point_region.astype(jnp.float32) / max(region_count - 1, 1)
    noise = 0.7 * jax.random.normal(noise_key, (SAMPLES, 3, PTS), jnp.float32)
    signal = jax.random.normal(signal_key, (SAMPLES, region_count), jnp.float32)
    loading = jax.random.normal(loading_key, (3, region_count), jnp.float32)
    rise = 0.6 + 0.6 * region_pos
    amplitude = jax.random.uniform(amp_key, (PTS,), jnp.float32, 0.5, 1.5) * rise
    signal_points = signal[:, point_region]
    loading_points = loading[:, point_region]
    coherent = signal_points[:, None, :] * loading_points[None, :, :] * amplitude[None, None, :]
    values = jnp.clip(noise + coherent, -6.0, 6.0)
    return values.astype(jnp.bfloat16)


def plant(array, own_key, least, high):
    longest = array.shape.index(max(array.shape))
    spots = []
    for shift in (0, 1):
        where = [jax.random.randint(jax.random.fold_in(own_key, axis), (), 0, length) for axis, length in enumerate(array.shape)]
        where[longest] = (where[longest] + shift) % array.shape[longest]
        spots.append(tuple(where))
    return array.at[spots[0]].set(least).at[spots[1]].set(high)


def block_levels(stream_key, extent, shards, smallest, top_value):
    gain, own = 1.0, jax.random.fold_in(stream_key, 6)
    for position, parts in shards:
        draws = jnp.exp(jax.random.uniform(jax.random.fold_in(own, position), (parts,), jnp.float32, smallest / len(shards), top_value / len(shards)))
        gain = gain * jnp.repeat(draws, extent[position] // parts).reshape([-1 if axis == position else 1 for axis in range(len(extent))])
    return gain


def setup_inputs(seed: int = 0) -> dict:
    arg_keys = jax.random.split(jax.random.key(seed), 4)
    return {
        "series": draw_series(jax.random.fold_in(arg_keys[3], 71), 0),
        "weights": jnp.clip(jnp.exp(math.log(0.00012207031) - 2.3025851 * jax.random.uniform(arg_keys[1], (PTS,), jnp.float32) ** block_levels(arg_keys[1], (PTS,), ((0, 8),), -0.2, 0.2)), 1.220703143189894e-05, 0.00012207031),
        "freq_bins": plant(jax.random.randint(arg_keys[2], (NF,), 1, NFFT // 2), jax.random.fold_in(arg_keys[2], 1), 1, (NFFT // 2) - 1).astype(jnp.int32),
    }


def build_table(freq_bins):
    sample_index = jnp.arange(NFFT, dtype=jnp.int32)
    window = (0.5 - 0.5 * jnp.cos(2.0 * jnp.pi * sample_index.astype(jnp.float32) / NFFT)) * jnp.sqrt(8.0 / (3.0 * NFFT))
    product_index = freq_bins[:, None] * sample_index[None, :] % NFFT
    phase_angle = 2.0 * jnp.pi * product_index.astype(jnp.float32) / NFFT
    kernel_table = jnp.stack([jnp.cos(phase_angle) * window, -jnp.sin(phase_angle) * window], axis=1)
    return kernel_table.reshape(2 * NF, NFFT).astype(jnp.bfloat16)

def matmul_high(left, right):
    return jnp.matmul(left, right, precision=lax.Precision.HIGHEST)

def combine(pair_gram):
    real_part = pair_gram[..., :NB, :NB] + pair_gram[..., NB:, NB:]
    imag_part = pair_gram[..., :NB, NB:] - pair_gram[..., NB:, :NB]
    return jnp.stack([real_part, imag_part], axis=-3)

def inverse_root(cross_gram):
    real_part = cross_gram[..., 0, :, :]
    imag_part = cross_gram[..., 1, :, :]
    norm_value = jnp.sqrt(lax.optimization_barrier(jnp.sum(cross_gram * cross_gram, axis=(-3, -2, -1))))
    upper_rows = jnp.concatenate([real_part, -imag_part], axis=-1)
    lower_rows = jnp.concatenate([imag_part, real_part], axis=-1)
    current = jnp.concatenate([upper_rows, lower_rows], axis=-2) / norm_value[..., None, None]
    identity = jnp.eye(2 * NB, dtype=jnp.float32)
    inv_root = jnp.broadcast_to(identity, current.shape)
    for iteration in range(ITERS):
        factor = 0.5 * (3.0 * identity - matmul_high(inv_root, current))
        current = matmul_high(current, factor)
        inv_root = matmul_high(factor, inv_root)
    return inv_root

def reference(series, weights, freq_bins):
    kernel_table = build_table(freq_bins)
    half_len = NFFT // 2
    halves = series.reshape(NB, half_len, 3 * PTS)

    def transform(segment):
        first_half = jnp.dot(kernel_table[:, :half_len], segment, preferred_element_type=jnp.float32)
        second_half = jnp.dot(kernel_table[:, half_len:], segment, preferred_element_type=jnp.float32)
        return (first_half, second_half)
    first_half, second_half = lax.map(transform, halves)
    coefficients = (first_half + jnp.roll(second_half, -1, axis=0)).astype(jnp.bfloat16)
    stacked = jnp.transpose(coefficients.reshape(NB, NF, 2, 3 * PTS), (1, 2, 0, 3)).reshape(NF, 2 * NB, 3 * PTS)
    row_weight = jnp.tile(weights, 3)

    def solve_bin(freq_rows):
        float_rows = freq_rows.astype(jnp.float32)
        pair_gram = jnp.dot(float_rows * row_weight[None, :], float_rows.T, precision=lax.Precision.HIGHEST)
        cross_gram = combine(pair_gram)
        inv_root = inverse_root(cross_gram).astype(jnp.bfloat16)
        spatial_modes = jnp.dot(inv_root, freq_rows, preferred_element_type=jnp.float32).astype(jnp.bfloat16)
        return (cross_gram, spatial_modes)
    cross_gram, spatial_modes = lax.map(solve_bin, stacked)
    return (cross_gram, spatial_modes.reshape(NF, 2, NB, 3, PTS))
```

```python
import functools

import jax
import jax.numpy as jnp
from jax import lax
from jax.experimental import pallas as pl
from jax.experimental.pallas import tpu as pltpu
from jax.sharding import PartitionSpec as P

NFFT = 512
NB = 32
NF = 16
ITERS = 4
HALF = NFFT // 2
UNIT = 256
MESH = pl.DeviceIdType.MESH
F32 = jnp.float32
BF16 = jnp.bfloat16


def half_wave(index):
    x = index.astype(F32) * F32(jnp.pi / 512.0)
    x2 = x * x
    c = F32(1.0 / 479001600.0)
    for v in (-1.0 / 3628800.0, 1.0 / 40320.0, -1.0 / 720.0, 1.0 / 24.0, -0.5, 1.0):
        c = c * x2 + F32(v)
    s = F32(-1.0 / 39916800.0)
    for v in (1.0 / 362880.0, -1.0 / 5040.0, 1.0 / 120.0, -1.0 / 6.0, 1.0):
        s = s * x2 + F32(v)
    return c, s * x


def build_table(freq_ref):
    shape = (2 * NF, HALF)
    row = lax.broadcasted_iota(jnp.int32, shape, 0)
    col = lax.broadcasted_iota(jnp.int32, shape, 1)
    freq = jnp.zeros(shape, jnp.int32)
    for f in range(NF):
        freq = jnp.where(row // 2 == f, freq_ref[f], freq)
    halves = []
    for h in range(2):
        n = col + h * HALF
        wc, _ = half_wave(n - HALF)
        window = wc * wc * F32((8.0 / (3.0 * NFFT)) ** 0.5)
        index = ((freq * n) & (NFFT - 1)) - HALF
        c, s = half_wave(index)
        cosine = 2.0 * s * s - 1.0
        minus_sine = 2.0 * s * c
        halves.append(jnp.where(row % 2 == 0, cosine, minus_sine) * window)
    return jnp.concatenate(halves, axis=0).astype(BF16)


def dot(left, right):
    return jnp.dot(left, right, preferred_element_type=F32)


def dot_t(left, right):
    return lax.dot_general(
        left, right, (((1,), (1,)), ((), ())), preferred_element_type=F32
    )


def split(value):
    hi = value.astype(BF16)
    return hi, (value - hi.astype(F32)).astype(BF16)


def dot_split(left, right):
    return dot(left[0], right[0]) + (dot(left[0], right[1]) + dot(left[1], right[0]))


def eye(size):
    row = lax.broadcasted_iota(jnp.int32, (size, size), 0)
    col = lax.broadcasted_iota(jnp.int32, (size, size), 1)
    return (row == col).astype(F32)


def normalized(real, imag):
    norm = jnp.sqrt(jnp.sum(real * real + imag * imag, axis=(0, 1), keepdims=True))
    upper = jnp.concatenate([real, -imag], axis=1)
    lower = jnp.concatenate([imag, real], axis=1)
    return jnp.concatenate([upper, lower], axis=0) * (1.0 / norm)


def inverse_roots(ys):
    half_three = 1.5 * eye(2 * NB)
    zs = None
    for it in range(ITERS):
        if zs is None:
            steps = [half_three - 0.5 * y for y in ys]
            ys = [dot_split(split(y), split(s)) for y, s in zip(ys, steps)]
            zs = steps
            continue
        zsp = [split(z) for z in zs]
        ysp = [split(y) for y in ys]
        steps = [half_three - 0.5 * dot_split(z, y) for z, y in zip(zsp, ysp)]
        ssp = [split(s) for s in steps]
        if it < ITERS - 1:
            ys = [dot_split(y, s) for y, s in zip(ysp, ssp)]
        zs = [dot_split(s, z) for s, z in zip(ssp, zsp)]
    return zs


def kernel(nt, ns, lf, series, freq, weights, cross_ref, modes_ref,
           xbuf, table, wbuf, fbuf, mid, edge, send, land, esend, eland, xall,
           out, ar, in_sem, small_sem, a_send, a_recv, e_send, e_recv,
           g_send, g_recv, out_sem):
    t = lax.axis_index("tm")
    s = lax.axis_index("pts")
    points = xbuf.shape[2]
    nq = points // UNIT
    nu = 3 * nq
    lanes = nu * UNIT
    lb = NB // nt
    per = 2 * lf
    rows = 2 * lb

    def series_copy(u):
        cols = pl.ds(u // 3 * UNIT, UNIT)
        return pltpu.make_async_copy(
            series.at[u % 3, :, cols], xbuf.at[u % 3, :, cols], in_sem.at[u]
        )

    freq_copy = pltpu.make_async_copy(freq, fbuf, small_sem.at[0])
    weight_copy = pltpu.make_async_copy(weights, wbuf, small_sem.at[1])
    freq_copy.start()
    for u in range(nu):
        series_copy(u).start()
    weight_copy.start()
    barrier = pltpu.get_barrier_semaphore()
    for k in range(1, nt):
        pl.semaphore_signal(barrier, inc=1, device_id={"tm": lax.rem(t + k, nt)},
                            device_id_type=MESH)
    for k in range(1, ns):
        pl.semaphore_signal(barrier, inc=1, device_id={"pts": lax.rem(s + k, ns)},
                            device_id_type=MESH)
    freq_copy.wait()
    table[...] = build_table(fbuf)

    early = lf // 2
    pieces = [(0, early, u, 1) for u in range(3)]
    pieces += [(0, early, u, 3) for u in range(3, nu, 3)]
    for f in range(early, lf):
        if f < lf - 1:
            pieces.append((f, 1, 0, nu))
        else:
            pieces += [(f, 1, 0, nu // 2), (f, 1, nu // 2, nu // 4),
                       (f, 1, nu // 2 + nu // 4, nu // 4)]

    def piece_copy(p, k):
        f, nf, u, n = pieces[p]
        to = lax.rem(t + k, nt)
        at = (pl.ds(f * rows, nf * rows), pl.ds(u * UNIT, n * UNIT))
        return pltpu.make_async_remote_copy(
            src_ref=send.at[(to, *at)], dst_ref=land.at[(k, *at)],
            send_sem=a_send.at[p, k], recv_sem=a_recv.at[p, k],
            device_id={"tm": to}, device_id_type=MESH,
        )

    def edge_copy(k):
        to = lax.rem(t + k, nt)
        return pltpu.make_async_remote_copy(
            src_ref=esend.at[to], dst_ref=eland.at[k],
            send_sem=e_send.at[k], recv_sem=e_recv.at[k],
            device_id={"tm": to}, device_id_type=MESH,
        )

    def gram_copy(f, k):
        return pltpu.make_async_remote_copy(
            src_ref=ar.at[f, 0], dst_ref=ar.at[f, k],
            send_sem=g_send.at[f, k], recv_sem=g_recv.at[f, k],
            device_id={"pts": lax.rem(s + k, ns)}, device_id_type=MESH,
        )

    def out_copy(f):
        return pltpu.make_async_copy(out.at[f], modes_ref.at[f], out_sem.at[f])

    def transform(u):
        series_copy(u).wait()
        cols = pl.ds(u // 3 * UNIT, UNIT)
        at = pl.ds(u * UNIT, UNIT)
        first = None
        for j in range(lb):
            both = dot(table[...], xbuf[u % 3, j * HALF:(j + 1) * HALF, cols])
            if j == 0:
                edge[:, at] = both[2 * NF:]
            else:
                value = first + both[2 * NF:]
                for v in range(UNIT // 128):
                    mid[v, pl.ds(j - 1, 2 * NF, stride=lb), :] = value[:, v * 128:(v + 1) * 128]
            first = both[:2 * NF]
        for v in range(UNIT // 128):
            mid[v, pl.ds(lb - 1, 2 * NF, stride=lb), :] = first[:, v * 128:(v + 1) * 128]
        for d in range(nt):
            for v in range(UNIT // 128):
                send[d, :, pl.ds(u * UNIT + v * 128, 128)] = mid[
                    v, d * lf * rows:(d + 1) * lf * rows, :].astype(BF16)
        land[0, :, at] = send[t, :, at]

    p = 0
    for u in range(nu):
        transform(u)
        if u == 0:
            pl.semaphore_wait(barrier, nt - 1 + ns - 1)
        if pieces[p][2] + pieces[p][3] == u + 1:
            for k in range(1, nt):
                piece_copy(p, k).start()
            p += 1
    for d in range(nt):
        e = edge[d * per:(d + 1) * per, :]
        esend[d] = jnp.concatenate([e[:, :lanes // 2], e[:, lanes // 2:]], axis=0).astype(BF16)
    for k in range(1, nt):
        edge_copy(k).start()
    for r in range(p, len(pieces)):
        for k in range(1, nt):
            piece_copy(r, k).start()
    eland[0] = esend[t]
    weight_copy.wait()

    last_row = lax.broadcasted_iota(jnp.int32, (lb, UNIT), 0) == lb - 1

    def unit_rows(f, u):
        at = pl.ds(u * UNIT, UNIT)
        half = u * UNIT // (lanes // 2)
        eat = pl.ds(u * UNIT - half * (lanes // 2), UNIT)
        parts = [[], []]
        for src in range(nt):
            x = land[lax.rem(t - src + nt, nt), f * rows:(f + 1) * rows, at].astype(F32)
            e = eland[lax.rem(t - src - 1 + nt, nt), :, eat].astype(F32)
            for i in range(2):
                r = half * per + 2 * f + i
                tail = jnp.where(last_row, e[r:r + 1], 0.0)
                parts[i].append(x[i * lb:(i + 1) * lb] + tail)
        return jnp.concatenate(parts[0] + parts[1], axis=0).astype(BF16)

    def gram(f, units, total):
        for u in units:
            x = unit_rows(f, u)
            xall[f, :, u * UNIT:(u + 1) * UNIT] = x
            w = wbuf[:, u // 3 * UNIT:(u // 3 + 1) * UNIT]
            xw = (x.astype(F32) * w).astype(BF16)
            part = dot_t(xw, x)
            total = part if total is None else total + part
        return total

    def share(f, pair):
        real = pair[:NB, :NB] + pair[NB:, NB:]
        imag = pair[:NB, NB:] - pair[NB:, :NB]
        h = NB // 2
        packed = jnp.concatenate([real[:h], imag[:h], real[h:], imag[h:]], axis=1)
        ar[f, 0] = packed.astype(BF16)
        for k in range(1, ns):
            gram_copy(f, k).start()

    def collect(f):
        for k in range(1, ns):
            gram_copy(f, k).wait_recv()
        total = None
        for src in range(ns):
            v = ar[f, lax.rem(s - src + ns, ns)].astype(F32)
            total = v if total is None else total + v
        real = jnp.concatenate([total[:, :NB], total[:, 2 * NB:3 * NB]], axis=0)
        imag = jnp.concatenate([total[:, NB:2 * NB], total[:, 3 * NB:]], axis=0)
        cross_ref[f, 0] = real
        cross_ref[f, 1] = imag
        return normalized(real, imag)

    def finish(bins):
        roots = inverse_roots([collect(f) for f in bins])
        for f, root in zip(bins, roots):
            root = root.astype(BF16)
            for u in range(nu):
                y = dot(root, xall[f, :, u * UNIT:(u + 1) * UNIT]).astype(BF16)
                cols = pl.ds(u // 3 * UNIT, UNIT)
                for i in range(2):
                    out[f, i, u % 3, :, cols] = y[i * NB:(i + 1) * NB]
            out_copy(f).start()

    def arrived(p):
        for k in range(1, nt):
            piece_copy(p, k).wait_recv()

    for k in range(1, nt):
        edge_copy(k).wait_recv()
    for r in range(p):
        arrived(r)
    for f in range(early):
        share(f, gram(f, range(nu), None))
    finish(range(early))
    for f in range(early, lf - 1):
        arrived(p)
        p += 1
        share(f, gram(f, range(nu), None))
    total = None
    for r in range(p, len(pieces)):
        arrived(r)
        _, _, u, n = pieces[r]
        total = gram(lf - 1, range(u, u + n), total)
    share(lf - 1, total)
    finish(range(early, lf - 1))
    finish([lf - 1])

    for r in range(len(pieces)):
        for k in range(1, nt):
            piece_copy(r, k).wait_send()
    for k in range(1, nt):
        edge_copy(k).wait_send()
    for f in range(lf):
        for k in range(1, ns):
            gram_copy(f, k).wait_send()
    for f in range(lf):
        out_copy(f).wait()


def on_device(nt, ns, series, weights, freq_bins):
    points = series.shape[2]
    nu = 3 * (points // UNIT)
    lanes = 3 * points
    lb, lf = NB // nt, NF // nt
    rows = 2 * lb
    n_pieces = 3 + nu // 3 - 1 + (lf - lf // 2 - 1) + 3
    hbm = pl.BlockSpec(memory_space=pl.ANY)
    vmem = pl.BlockSpec(memory_space=pltpu.VMEM)
    cross, modes = pl.pallas_call(
        functools.partial(kernel, nt, ns, lf),
        out_shape=(
            jax.ShapeDtypeStruct((lf, 2, NB, NB), F32),
            jax.ShapeDtypeStruct((lf, 2, 3, NB, points), BF16),
        ),
        in_specs=[hbm, hbm, hbm],
        out_specs=(vmem, hbm),
        scratch_shapes=[
            pltpu.VMEM((3, series.shape[0], points), BF16),
            pltpu.VMEM((4 * NF, HALF), BF16),
            pltpu.VMEM((1, points), F32),
            pltpu.SMEM((NF,), jnp.int32),
            pltpu.VMEM((UNIT // 128, 2 * NF * lb, 128), F32),
            pltpu.VMEM((2 * NF, lanes), F32),
            pltpu.VMEM((nt, lf * rows, lanes), BF16),
            pltpu.VMEM((nt, lf * rows, lanes), BF16),
            pltpu.VMEM((nt, 4 * lf, lanes // 2), BF16),
            pltpu.VMEM((nt, 4 * lf, lanes // 2), BF16),
            pltpu.VMEM((lf, 2 * NB, lanes), BF16),
            pltpu.VMEM((lf, 2, 3, NB, points), BF16),
            pltpu.VMEM((lf, ns, NB // 2, 4 * NB), BF16),
            pltpu.SemaphoreType.DMA((nu,)),
            pltpu.SemaphoreType.DMA((2,)),
            pltpu.SemaphoreType.DMA((n_pieces, nt)),
            pltpu.SemaphoreType.DMA((n_pieces, nt)),
            pltpu.SemaphoreType.DMA((nt,)),
            pltpu.SemaphoreType.DMA((nt,)),
            pltpu.SemaphoreType.DMA((lf, ns)),
            pltpu.SemaphoreType.DMA((lf, ns)),
            pltpu.SemaphoreType.DMA((lf,)),
        ],
        compiler_params=pltpu.CompilerParams(
            collective_id=0, has_side_effects=True, vmem_limit_bytes=54 * 2**20
        ),
    )(series.transpose(1, 0, 2), freq_bins, weights.reshape(1, points))
    return cross, modes.transpose(0, 1, 3, 2, 4)


def solution(mesh):
    nt, ns = mesh.shape["tm"], mesh.shape["pts"]
    in_specs = (P("tm", None, "pts"), P("pts"), P())
    out_specs = (P("tm", None, None, None), P("tm", None, None, None, "pts"))
    return jax.shard_map(
        functools.partial(on_device, nt, ns), mesh=mesh, in_specs=in_specs,
        out_specs=out_specs, check_vma=False
    )
```

```python
import functools

import jax
import jax.numpy as jnp
from jax import lax
from jax.experimental import pallas as pl
from jax.experimental.pallas import tpu as pltpu
from jax.sharding import PartitionSpec as P

NFFT = 512
NB = 32
NF = 16
ITERS = 4
HALF = NFFT // 2
UNIT = 256
MESH = pl.DeviceIdType.MESH
F32 = jnp.float32
BF16 = jnp.bfloat16


def half_wave(index):
    x = index.astype(F32) * F32(jnp.pi / 512.0)
    x2 = x * x
    c = F32(1.0 / 479001600.0)
    for v in (-1.0 / 3628800.0, 1.0 / 40320.0, -1.0 / 720.0, 1.0 / 24.0, -0.5, 1.0):
        c = c * x2 + F32(v)
    s = F32(-1.0 / 39916800.0)
    for v in (1.0 / 362880.0, -1.0 / 5040.0, 1.0 / 120.0, -1.0 / 6.0, 1.0):
        s = s * x2 + F32(v)
    return c, s * x


def build_table(freq_ref):
    shape = (2 * NF, HALF)
    row = lax.broadcasted_iota(jnp.int32, shape, 0)
    col = lax.broadcasted_iota(jnp.int32, shape, 1)
    freq = jnp.zeros(shape, jnp.int32)
    for f in range(NF):
        freq = jnp.where(row // 2 == f, freq_ref[f], freq)
    halves = []
    for h in range(2):
        n = col + h * HALF
        wc, _ = half_wave(n - HALF)
        window = wc * wc * F32((8.0 / (3.0 * NFFT)) ** 0.5)
        index = ((freq * n) & (NFFT - 1)) - HALF
        c, s = half_wave(index)
        cosine = 2.0 * s * s - 1.0
        minus_sine = 2.0 * s * c
        halves.append(jnp.where(row % 2 == 0, cosine, minus_sine) * window)
    return jnp.concatenate(halves, axis=0).astype(BF16)


def dot(left, right):
    return jnp.dot(left, right, preferred_element_type=F32)


def dot_t(left, right):
    return lax.dot_general(
        left, right, (((1,), (1,)), ((), ())), preferred_element_type=F32
    )


def split(value):
    hi = value.astype(BF16)
    return hi, (value - hi.astype(F32)).astype(BF16)


def dot_split(left, right):
    return dot(left[0], right[0]) + (dot(left[0], right[1]) + dot(left[1], right[0]))


def eye(size):
    row = lax.broadcasted_iota(jnp.int32, (size, size), 0)
    col = lax.broadcasted_iota(jnp.int32, (size, size), 1)
    return (row == col).astype(F32)


def normalized(real, imag):
    norm = jnp.sqrt(jnp.sum(real * real + imag * imag, axis=(0, 1), keepdims=True))
    upper = jnp.concatenate([real, -imag], axis=1)
    lower = jnp.concatenate([imag, real], axis=1)
    return jnp.concatenate([upper, lower], axis=0) * (1.0 / norm)


def inverse_roots(ys):
    half_three = 1.5 * eye(2 * NB)
    zs = None
    for it in range(ITERS):
        if zs is None:
            steps = [half_three - 0.5 * y for y in ys]
            ys = [dot_split(split(y), split(s)) for y, s in zip(ys, steps)]
            zs = steps
            continue
        zsp = [split(z) for z in zs]
        ysp = [split(y) for y in ys]
        steps = [half_three - 0.5 * dot_split(z, y) for z, y in zip(zsp, ysp)]
        ssp = [split(s) for s in steps]
        if it < ITERS - 1:
            ys = [dot_split(y, s) for y, s in zip(ysp, ssp)]
        zs = [dot_split(s, z) for s, z in zip(ssp, zsp)]
    return zs


def mix(root, rows_of, out, nu):
    for u in range(nu):
        y = dot(root, rows_of(u)).astype(BF16)
        cols = pl.ds(u // 3 * UNIT, UNIT)
        for i in range(2):
            out[i, u % 3, :, cols] = y[i * NB:(i + 1) * NB]


def finish_kernel(nu, cross_in, early, x, cross_ref, modes_ref,
                  out, early_sem, out_sem):
    lf = cross_in.shape[0]
    copies = [
        pltpu.make_async_copy(early.at[f], modes_ref.at[f], early_sem.at[f])
        for f in range(lf - 1)
    ]
    for c in copies:
        c.start()
    cross_ref[...] = cross_in[...]
    y = normalized(cross_in[lf - 1, 0], cross_in[lf - 1, 1])
    (root,) = inverse_roots([y])
    mix(root.astype(BF16), lambda u: x[:, u * UNIT:(u + 1) * UNIT], out, nu)
    copies.append(pltpu.make_async_copy(out, modes_ref.at[lf - 1], out_sem))
    copies[-1].start()
    for c in copies:
        c.wait()


def kernel(nt, ns, lf, series, freq, weights, cross_ref, early_ref, x_ref,
           xbuf, table, wbuf, fbuf, mid, edge, send, land, esend, eland, xall,
           ar, in_sem, small_sem, a_send, a_recv, e_send, e_recv,
           g_send, g_recv):
    t = lax.axis_index("tm")
    s = lax.axis_index("pts")
    points = xbuf.shape[2]
    nq = points // UNIT
    nu = 3 * nq
    lanes = nu * UNIT
    lb = NB // nt
    per = 2 * lf
    rows = 2 * lb

    def series_copy(u):
        cols = pl.ds(u // 3 * UNIT, UNIT)
        return pltpu.make_async_copy(
            series.at[u % 3, :, cols], xbuf.at[u % 3, :, cols], in_sem.at[u]
        )

    freq_copy = pltpu.make_async_copy(freq, fbuf, small_sem.at[0])
    weight_copy = pltpu.make_async_copy(weights, wbuf, small_sem.at[1])
    freq_copy.start()
    for u in range(3):
        series_copy(u).start()
    barrier = pltpu.get_barrier_semaphore()
    for k in range(1, nt):
        pl.semaphore_signal(barrier, inc=1, device_id={"tm": lax.rem(t + k, nt)},
                            device_id_type=MESH)
    for k in range(1, ns):
        pl.semaphore_signal(barrier, inc=1, device_id={"pts": lax.rem(s + k, ns)},
                            device_id_type=MESH)
    for u in range(3, nu):
        series_copy(u).start()
    weight_copy.start()
    freq_copy.wait()
    table[...] = build_table(fbuf)

    early = lf // 2
    pieces = [(0, early, u, 1) for u in range(3)]
    pieces += [(0, early, u, 3) for u in range(3, nu, 3)]
    for f in range(early, lf):
        if f < lf - 1:
            pieces.append((f, 1, 0, nu))
        else:
            pieces += [(f, 1, 0, nu // 2), (f, 1, nu // 2, nu // 4),
                       (f, 1, nu // 2 + nu // 4, nu // 4)]

    def piece_copy(p, k):
        f, nf, u, n = pieces[p]
        to = lax.rem(t + k, nt)
        at = (pl.ds(f * rows, nf * rows), pl.ds(u * UNIT, n * UNIT))
        return pltpu.make_async_remote_copy(
            src_ref=send.at[(to, *at)], dst_ref=land.at[(k, *at)],
            send_sem=a_send.at[p, k], recv_sem=a_recv.at[p, k],
            device_id={"tm": to}, device_id_type=MESH,
        )

    def edge_copy(k):
        to = lax.rem(t + k, nt)
        return pltpu.make_async_remote_copy(
            src_ref=esend.at[to], dst_ref=eland.at[k],
            send_sem=e_send.at[k], recv_sem=e_recv.at[k],
            device_id={"tm": to}, device_id_type=MESH,
        )

    def gram_copy(f, k):
        return pltpu.make_async_remote_copy(
            src_ref=ar.at[f, 0], dst_ref=ar.at[f, k],
            send_sem=g_send.at[f, k], recv_sem=g_recv.at[f, k],
            device_id={"pts": lax.rem(s + k, ns)}, device_id_type=MESH,
        )

    def rows_of(f):
        return xall.at[f] if f < lf - 1 else x_ref

    def transform(u):
        series_copy(u).wait()
        cols = pl.ds(u // 3 * UNIT, UNIT)
        at = pl.ds(u * UNIT, UNIT)
        first = None
        for j in range(lb):
            both = dot(table[...], xbuf[u % 3, j * HALF:(j + 1) * HALF, cols])
            if j == 0:
                edge[:, at] = both[2 * NF:]
            else:
                value = first + both[2 * NF:]
                for v in range(UNIT // 128):
                    mid[v, pl.ds(j - 1, 2 * NF, stride=lb), :] = value[:, v * 128:(v + 1) * 128]
            first = both[:2 * NF]
        for v in range(UNIT // 128):
            mid[v, pl.ds(lb - 1, 2 * NF, stride=lb), :] = first[:, v * 128:(v + 1) * 128]
        for d in range(nt):
            for v in range(UNIT // 128):
                send[d, :, pl.ds(u * UNIT + v * 128, 128)] = mid[
                    v, d * lf * rows:(d + 1) * lf * rows, :].astype(BF16)
        land[0, :, at] = send[t, :, at]

    p = 0
    for u in range(nu):
        transform(u)
        if u == 0:
            pl.semaphore_wait(barrier, nt - 1 + ns - 1)
        if pieces[p][2] + pieces[p][3] == u + 1:
            for k in range(1, nt):
                piece_copy(p, k).start()
            p += 1
    for d in range(nt):
        e = edge[d * per:(d + 1) * per, :]
        esend[d] = jnp.concatenate([e[:, :lanes // 2], e[:, lanes // 2:]], axis=0).astype(BF16)
    for k in range(1, nt):
        edge_copy(k).start()
    def begin(r):
        for k in range(1, nt):
            piece_copy(r, k).start()

    begin(p)
    eland[0] = esend[t]
    weight_copy.wait()

    last_row = lax.broadcasted_iota(jnp.int32, (lb, UNIT), 0) == lb - 1

    def unit_rows(f, u):
        at = pl.ds(u * UNIT, UNIT)
        half = u * UNIT // (lanes // 2)
        eat = pl.ds(u * UNIT - half * (lanes // 2), UNIT)
        parts = [[], []]
        for src in range(nt):
            x = land[lax.rem(t - src + nt, nt), f * rows:(f + 1) * rows, at].astype(F32)
            e = eland[lax.rem(t - src - 1 + nt, nt), :, eat].astype(F32)
            for i in range(2):
                r = half * per + 2 * f + i
                tail = jnp.where(last_row, e[r:r + 1], 0.0)
                parts[i].append(x[i * lb:(i + 1) * lb] + tail)
        return jnp.concatenate(parts[0] + parts[1], axis=0).astype(BF16)

    def gram(f, units, total):
        for u in units:
            x = unit_rows(f, u)
            rows_of(f)[:, u * UNIT:(u + 1) * UNIT] = x
            w = wbuf[:, u // 3 * UNIT:(u // 3 + 1) * UNIT]
            xw = (x.astype(F32) * w).astype(BF16)
            part = dot_t(xw, x)
            total = part if total is None else total + part
        return total

    def share(f, pair):
        real = pair[:NB, :NB] + pair[NB:, NB:]
        imag = pair[:NB, NB:] - pair[NB:, :NB]
        h = NB // 2
        packed = jnp.concatenate([real[:h], imag[:h], real[h:], imag[h:]], axis=1)
        ar[f, 0] = packed.astype(BF16)
        for k in range(1, ns):
            gram_copy(f, k).start()

    def collect(f):
        for k in range(1, ns):
            gram_copy(f, k).wait_recv()
        total = None
        for src in range(ns):
            v = ar[f, lax.rem(s - src + ns, ns)].astype(F32)
            total = v if total is None else total + v
        real = jnp.concatenate([total[:, :NB], total[:, 2 * NB:3 * NB]], axis=0)
        imag = jnp.concatenate([total[:, NB:2 * NB], total[:, 3 * NB:]], axis=0)
        cross_ref[f, 0] = real
        cross_ref[f, 1] = imag
        return real, imag

    def finish(bins):
        roots = inverse_roots([normalized(*collect(f)) for f in bins])
        for f, root in zip(bins, roots):
            mix(root.astype(BF16), lambda u: xall[f, :, u * UNIT:(u + 1) * UNIT],
                early_ref.at[f], nu)

    def arrived(p):
        for k in range(1, nt):
            piece_copy(p, k).wait_recv()

    for k in range(1, nt):
        edge_copy(k).wait_recv()
    for r in range(p):
        arrived(r)
    for f in range(early):
        share(f, gram(f, range(nu), None))
    begin(p + 1)
    for f in range(early, lf - 1):
        arrived(p)
        p += 1
        share(f, gram(f, range(nu), None))
        if f < lf - 2:
            begin(p + 1)
    for r in range(p + 1, len(pieces)):
        begin(r)
    finish(range(early))
    total = None
    for r in range(p, len(pieces)):
        arrived(r)
        _, _, u, n = pieces[r]
        total = gram(lf - 1, range(u, u + n), total)
    share(lf - 1, total)
    finish(range(early, lf - 1))
    collect(lf - 1)

    for r in range(len(pieces)):
        for k in range(1, nt):
            piece_copy(r, k).wait_send()
    for k in range(1, nt):
        edge_copy(k).wait_send()
    for f in range(lf):
        for k in range(1, ns):
            gram_copy(f, k).wait_send()


def on_device(nt, ns, series, weights, freq_bins):
    points = series.shape[2]
    nu = 3 * (points // UNIT)
    lanes = 3 * points
    lb, lf = NB // nt, NF // nt
    rows = 2 * lb
    n_pieces = 3 + nu // 3 - 1 + (lf - lf // 2 - 1) + 3
    hbm = pl.BlockSpec(memory_space=pl.ANY)
    vmem = pl.BlockSpec(memory_space=pltpu.VMEM)
    cross, early, x = pl.pallas_call(
        functools.partial(kernel, nt, ns, lf),
        out_shape=(
            jax.ShapeDtypeStruct((lf, 2, NB, NB), F32),
            jax.ShapeDtypeStruct((lf - 1, 2, 3, NB, points), BF16),
            jax.ShapeDtypeStruct((2 * NB, lanes), BF16),
        ),
        in_specs=[hbm, hbm, hbm],
        out_specs=(vmem, vmem, vmem),
        scratch_shapes=[
            pltpu.VMEM((3, series.shape[0], points), BF16),
            pltpu.VMEM((4 * NF, HALF), BF16),
            pltpu.VMEM((1, points), F32),
            pltpu.SMEM((NF,), jnp.int32),
            pltpu.VMEM((UNIT // 128, 2 * NF * lb, 128), F32),
            pltpu.VMEM((2 * NF, lanes), F32),
            pltpu.VMEM((nt, lf * rows, lanes), BF16),
            pltpu.VMEM((nt, lf * rows, lanes), BF16),
            pltpu.VMEM((nt, 4 * lf, lanes // 2), BF16),
            pltpu.VMEM((nt, 4 * lf, lanes // 2), BF16),
            pltpu.VMEM((lf - 1, 2 * NB, lanes), BF16),
            pltpu.VMEM((lf, ns, NB // 2, 4 * NB), BF16),
            pltpu.SemaphoreType.DMA((nu,)),
            pltpu.SemaphoreType.DMA((2,)),
            pltpu.SemaphoreType.DMA((n_pieces, nt)),
            pltpu.SemaphoreType.DMA((n_pieces, nt)),
            pltpu.SemaphoreType.DMA((nt,)),
            pltpu.SemaphoreType.DMA((nt,)),
            pltpu.SemaphoreType.DMA((lf, ns)),
            pltpu.SemaphoreType.DMA((lf, ns)),
        ],
        compiler_params=pltpu.CompilerParams(
            collective_id=0, has_side_effects=True, vmem_limit_bytes=50 * 2**20
        ),
    )(*(pltpu.with_memory_space_constraint(v, pltpu.HBM)
        for v in (series.transpose(1, 0, 2), freq_bins, weights.reshape(1, points))))
    cross, modes = pl.pallas_call(
        functools.partial(finish_kernel, nu),
        out_shape=(
            jax.ShapeDtypeStruct((lf, 2, NB, NB), F32),
            jax.ShapeDtypeStruct((lf, 2, 3, NB, points), BF16),
        ),
        in_specs=[vmem, vmem, vmem],
        out_specs=(vmem, hbm),
        scratch_shapes=[
            pltpu.VMEM((2, 3, NB, points), BF16),
            pltpu.SemaphoreType.DMA((lf - 1,)),
            pltpu.SemaphoreType.DMA,
        ],
        compiler_params=pltpu.CompilerParams(vmem_limit_bytes=16 * 2**20),
    )(cross, early, x)
    return cross, modes.transpose(0, 1, 3, 2, 4)


def solution(mesh):
    nt, ns = mesh.shape["tm"], mesh.shape["pts"]
    in_specs = (P("tm", None, "pts"), P("pts"), P())
    out_specs = (P("tm", None, None, None), P("tm", None, None, None, "pts"))
    return jax.shard_map(
        functools.partial(on_device, nt, ns), mesh=mesh, in_specs=in_specs,
        out_specs=out_specs, check_vma=False
    )
```

```python
import functools

import jax
import jax.numpy as jnp
from jax import lax
from jax.experimental import pallas as pl
from jax.experimental.pallas import tpu as pltpu
from jax.sharding import PartitionSpec as P

NFFT = 512
NB = 32
NF = 16
ITERS = 4
HALF = NFFT // 2
UNIT = 256
MESH = pl.DeviceIdType.MESH
F32 = jnp.float32
BF16 = jnp.bfloat16


def half_wave(index):
    x = index.astype(F32) * F32(jnp.pi / 512.0)
    x2 = x * x
    c = F32(1.0 / 479001600.0)
    for v in (-1.0 / 3628800.0, 1.0 / 40320.0, -1.0 / 720.0, 1.0 / 24.0, -0.5, 1.0):
        c = c * x2 + F32(v)
    s = F32(-1.0 / 39916800.0)
    for v in (1.0 / 362880.0, -1.0 / 5040.0, 1.0 / 120.0, -1.0 / 6.0, 1.0):
        s = s * x2 + F32(v)
    return c, s * x


def build_table(freq_ref):
    shape = (2 * NF, HALF)
    row = lax.broadcasted_iota(jnp.int32, shape, 0)
    col = lax.broadcasted_iota(jnp.int32, shape, 1)
    freq = jnp.zeros(shape, jnp.int32)
    for f in range(NF):
        freq = jnp.where(row // 2 == f, freq_ref[f], freq)
    halves = []
    for h in range(2):
        n = col + h * HALF
        wc, _ = half_wave(n - HALF)
        window = wc * wc * F32((8.0 / (3.0 * NFFT)) ** 0.5)
        index = ((freq * n) & (NFFT - 1)) - HALF
        c, s = half_wave(index)
        cosine = 2.0 * s * s - 1.0
        minus_sine = 2.0 * s * c
        halves.append(jnp.where(row % 2 == 0, cosine, minus_sine) * window)
    return jnp.concatenate(halves, axis=0).astype(BF16)


def dot(left, right):
    return jnp.dot(left, right, preferred_element_type=F32)


def dot_t(left, right):
    return lax.dot_general(
        left, right, (((1,), (1,)), ((), ())), preferred_element_type=F32
    )


def split(value):
    hi = value.astype(BF16)
    return hi, (value - hi.astype(F32)).astype(BF16)


def dot_split(left, right):
    return dot(left[0], right[0]) + (dot(left[0], right[1]) + dot(left[1], right[0]))


def eye(size):
    row = lax.broadcasted_iota(jnp.int32, (size, size), 0)
    col = lax.broadcasted_iota(jnp.int32, (size, size), 1)
    return (row == col).astype(F32)


def normalized(real, imag):
    norm = jnp.sqrt(jnp.sum(real * real + imag * imag, axis=(0, 1), keepdims=True))
    upper = jnp.concatenate([real, -imag], axis=1)
    lower = jnp.concatenate([imag, real], axis=1)
    return jnp.concatenate([upper, lower], axis=0) * (1.0 / norm)


def inverse_roots(ys):
    half_three = 1.5 * eye(2 * NB)
    zs = None
    for it in range(ITERS):
        if zs is None:
            steps = [half_three - 0.5 * y for y in ys]
            ys = [dot_split(split(y), split(s)) for y, s in zip(ys, steps)]
            zs = steps
            continue
        zsp = [split(z) for z in zs]
        ysp = [split(y) for y in ys]
        steps = [half_three - 0.5 * dot_split(z, y) for z, y in zip(zsp, ysp)]
        ssp = [split(s) for s in steps]
        if it < ITERS - 1:
            ys = [dot_split(y, s) for y, s in zip(ysp, ssp)]
        zs = [dot_split(s, z) for s, z in zip(ssp, zsp)]
    return zs


def mix(root, rows_of, out, nu):
    for u in range(nu):
        y = dot(root, rows_of(u)).astype(BF16)
        cols = pl.ds(u // 3 * UNIT, UNIT)
        for i in range(2):
            out[i, u % 3, :, cols] = y[i * NB:(i + 1) * NB]


def finish_kernel(nu, cross_in, early, x, cross_ref, modes_ref,
                  out, early_sem, out_sem, cross_sem):
    lf = cross_in.shape[0]
    copies = [pltpu.make_async_copy(cross_in, cross_ref, cross_sem)]
    copies += [
        pltpu.make_async_copy(early.at[f], modes_ref.at[f], early_sem.at[f])
        for f in range(lf - 1)
    ]
    for c in copies:
        c.start()
    y = normalized(cross_in[lf - 1, 0], cross_in[lf - 1, 1])
    (root,) = inverse_roots([y])
    mix(root.astype(BF16), lambda u: x[:, u * UNIT:(u + 1) * UNIT], out, nu)
    copies.append(pltpu.make_async_copy(out, modes_ref.at[lf - 1], out_sem))
    copies[-1].start()
    for c in copies:
        c.wait()


def kernel(nt, ns, lf, series, freq, weights, cross_ref, early_ref, x_ref,
           xbuf, table, wbuf, fbuf, mid, edge, send, land, esend, eland, xall,
           ar, in_sem, small_sem, a_send, a_recv, e_send, e_recv,
           g_send, g_recv, go_sem):
    t = lax.axis_index("tm")
    s = lax.axis_index("pts")
    points = xbuf.shape[2]
    nq = points // UNIT
    nu = 3 * nq
    lanes = nu * UNIT
    lb = NB // nt
    per = 2 * lf
    rows = 2 * lb

    def series_copy(u):
        cols = pl.ds(u // 3 * UNIT, UNIT)
        return pltpu.make_async_copy(
            series.at[u % 3, :, cols], xbuf.at[u % 3, :, cols], in_sem.at[u]
        )

    freq_copy = pltpu.make_async_copy(freq, fbuf, small_sem.at[0])
    weight_copy = pltpu.make_async_copy(weights, wbuf, small_sem.at[1])
    freq_copy.start()
    for u in range(3):
        series_copy(u).start()
    barrier = pltpu.get_barrier_semaphore()
    for k in range(1, nt):
        pl.semaphore_signal(barrier, inc=1, device_id={"tm": lax.rem(t + k, nt)},
                            device_id_type=MESH)
    root = ns // 2

    @pl.when(s != root)
    def _():
        pl.semaphore_signal(barrier, inc=1, device_id={"pts": root}, device_id_type=MESH)

    for u in range(3, nu):
        series_copy(u).start()
    weight_copy.start()
    freq_copy.wait()
    table[...] = build_table(fbuf)

    early = lf // 2
    pieces = [(0, early, u, 1) for u in range(3)]
    pieces += [(0, early, u, 3) for u in range(3, nu, 3)]
    for f in range(early, lf):
        if f < lf - 1:
            pieces.append((f, 1, 0, nu))
        else:
            pieces += [(f, 1, 0, nu - nu // 4), (f, 1, nu - nu // 4, nu // 4)]

    def piece_copy(p, k):
        f, nf, u, n = pieces[p]
        to = lax.rem(t + k, nt)
        at = (pl.ds(f * rows, nf * rows), pl.ds(u * UNIT, n * UNIT))
        return pltpu.make_async_remote_copy(
            src_ref=send.at[(to, *at)], dst_ref=land.at[(k, *at)],
            send_sem=a_send.at[p, k], recv_sem=a_recv.at[p, k],
            device_id={"tm": to}, device_id_type=MESH,
        )

    def edge_copy(k):
        to = lax.rem(t + k, nt)
        return pltpu.make_async_remote_copy(
            src_ref=esend.at[to], dst_ref=eland.at[k],
            send_sem=e_send.at[k], recv_sem=e_recv.at[k],
            device_id={"tm": to}, device_id_type=MESH,
        )

    def gram_copy(f, k):
        return pltpu.make_async_remote_copy(
            src_ref=ar.at[f, 0], dst_ref=ar.at[f, k],
            send_sem=g_send.at[f, k], recv_sem=g_recv.at[f, k],
            device_id={"pts": lax.rem(s + k, ns)}, device_id_type=MESH,
        )

    def rows_of(f):
        return xall.at[f] if f < lf - 1 else x_ref

    def transform(u):
        series_copy(u).wait()
        cols = pl.ds(u // 3 * UNIT, UNIT)
        at = pl.ds(u * UNIT, UNIT)
        first = None
        for j in range(lb):
            both = dot(table[...], xbuf[u % 3, j * HALF:(j + 1) * HALF, cols])
            if j == 0:
                edge[:, at] = both[2 * NF:]
            else:
                value = first + both[2 * NF:]
                for v in range(UNIT // 128):
                    mid[v, pl.ds(j - 1, 2 * NF, stride=lb), :] = value[:, v * 128:(v + 1) * 128]
            first = both[:2 * NF]
        for v in range(UNIT // 128):
            mid[v, pl.ds(lb - 1, 2 * NF, stride=lb), :] = first[:, v * 128:(v + 1) * 128]
        for d in range(nt):
            for v in range(UNIT // 128):
                send[d, :, pl.ds(u * UNIT + v * 128, 128)] = mid[
                    v, d * lf * rows:(d + 1) * lf * rows, :].astype(BF16)
        land[0, :, at] = send[t, :, at]

    p = 0
    for u in range(nu):
        transform(u)
        if u == 0:
            pl.semaphore_wait(barrier, nt - 1 + jnp.where(s == root, ns - 1, 0))

            @pl.when(s == root)
            def _():
                for k in range(1, ns):
                    pl.semaphore_signal(go_sem, inc=1, device_id={"pts": lax.rem(s + k, ns)},
                                        device_id_type=MESH)
        if pieces[p][2] + pieces[p][3] == u + 1:
            for k in range(1, nt):
                piece_copy(p, k).start()
            p += 1
    for d in range(nt):
        e = edge[d * per:(d + 1) * per, :]
        esend[d] = jnp.concatenate([e[:, :lanes // 2], e[:, lanes // 2:]], axis=0).astype(BF16)
    for k in range(1, nt):
        edge_copy(k).start()
    def begin(r):
        for k in range(1, nt):
            piece_copy(r, k).start()

    begin(p)
    eland[0] = esend[t]
    weight_copy.wait()

    last_row = lax.broadcasted_iota(jnp.int32, (lb, UNIT), 0) == lb - 1

    def unit_rows(f, u):
        at = pl.ds(u * UNIT, UNIT)
        half = u * UNIT // (lanes // 2)
        eat = pl.ds(u * UNIT - half * (lanes // 2), UNIT)
        parts = [[], []]
        for src in range(nt):
            x = land[lax.rem(t - src + nt, nt), f * rows:(f + 1) * rows, at].astype(F32)
            e = eland[lax.rem(t - src - 1 + nt, nt), :, eat].astype(F32)
            for i in range(2):
                r = half * per + 2 * f + i
                tail = jnp.where(last_row, e[r:r + 1], 0.0)
                parts[i].append(x[i * lb:(i + 1) * lb] + tail)
        return jnp.concatenate(parts[0] + parts[1], axis=0).astype(BF16)

    def gram(f, units, total):
        for u in units:
            x = unit_rows(f, u)
            rows_of(f)[:, u * UNIT:(u + 1) * UNIT] = x
            w = wbuf[:, u // 3 * UNIT:(u // 3 + 1) * UNIT]
            xw = (x.astype(F32) * w).astype(BF16)
            part = dot_t(xw, x)
            total = part if total is None else total + part
        return total

    def share(f, pair):
        real = pair[:NB, :NB] + pair[NB:, NB:]
        imag = pair[:NB, NB:] - pair[NB:, :NB]
        h = NB // 2
        packed = jnp.concatenate([real[:h], imag[:h], real[h:], imag[h:]], axis=1)
        ar[f, 0] = packed.astype(BF16)
        for k in range(1, ns):
            gram_copy(f, k).start()

    def collect(f):
        for k in range(1, ns):
            gram_copy(f, k).wait_recv()
        total = None
        for src in range(ns):
            v = ar[f, lax.rem(s - src + ns, ns)].astype(F32)
            total = v if total is None else total + v
        real = jnp.concatenate([total[:, :NB], total[:, 2 * NB:3 * NB]], axis=0)
        imag = jnp.concatenate([total[:, NB:2 * NB], total[:, 3 * NB:]], axis=0)
        cross_ref[f, 0] = real
        cross_ref[f, 1] = imag
        return real, imag

    def finish(bins):
        roots = inverse_roots([normalized(*collect(f)) for f in bins])
        for f, root in zip(bins, roots):
            mix(root.astype(BF16), lambda u: xall[f, :, u * UNIT:(u + 1) * UNIT],
                early_ref.at[f], nu)

    def arrived(p):
        for k in range(1, nt):
            piece_copy(p, k).wait_recv()

    for k in range(1, nt):
        edge_copy(k).wait_recv()
    for r in range(p):
        arrived(r)
    grams = [gram(f, range(nu), None) for f in range(early)]

    @pl.when(s != root)
    def _():
        pl.semaphore_wait(go_sem, 1)

    for f in range(early):
        share(f, grams[f])
    begin(p + 1)
    for f in range(early, lf - 1):
        arrived(p)
        p += 1
        share(f, gram(f, range(nu), None))
        if f < lf - 2:
            begin(p + 1)
    for r in range(p + 1, len(pieces)):
        begin(r)
    finish(range(early))
    total = None
    for r in range(p, len(pieces)):
        arrived(r)
        _, _, u, n = pieces[r]
        total = gram(lf - 1, range(u, u + n), total)
    share(lf - 1, total)
    finish(range(early, lf - 1))
    collect(lf - 1)

    for r in range(len(pieces)):
        for k in range(1, nt):
            piece_copy(r, k).wait_send()
    for k in range(1, nt):
        edge_copy(k).wait_send()
    for f in range(lf):
        for k in range(1, ns):
            gram_copy(f, k).wait_send()


def on_device(nt, ns, series, weights, freq_bins):
    points = series.shape[2]
    nu = 3 * (points // UNIT)
    lanes = 3 * points
    lb, lf = NB // nt, NF // nt
    rows = 2 * lb
    n_pieces = 3 + nu // 3 - 1 + (lf - lf // 2 - 1) + 2
    hbm = pl.BlockSpec(memory_space=pl.ANY)
    vmem = pl.BlockSpec(memory_space=pltpu.VMEM)
    cross, early, x = pl.pallas_call(
        functools.partial(kernel, nt, ns, lf),
        out_shape=(
            jax.ShapeDtypeStruct((lf, 2, NB, NB), F32),
            jax.ShapeDtypeStruct((lf - 1, 2, 3, NB, points), BF16),
            jax.ShapeDtypeStruct((2 * NB, lanes), BF16),
        ),
        in_specs=[hbm, hbm, hbm],
        out_specs=(vmem, vmem, vmem),
        scratch_shapes=[
            pltpu.VMEM((3, series.shape[0], points), BF16),
            pltpu.VMEM((4 * NF, HALF), BF16),
            pltpu.VMEM((1, points), F32),
            pltpu.SMEM((NF,), jnp.int32),
            pltpu.VMEM((UNIT // 128, 2 * NF * lb, 128), F32),
            pltpu.VMEM((2 * NF, lanes), F32),
            pltpu.VMEM((nt, lf * rows, lanes), BF16),
            pltpu.VMEM((nt, lf * rows, lanes), BF16),
            pltpu.VMEM((nt, 4 * lf, lanes // 2), BF16),
            pltpu.VMEM((nt, 4 * lf, lanes // 2), BF16),
            pltpu.VMEM((lf - 1, 2 * NB, lanes), BF16),
            pltpu.VMEM((lf, ns, NB // 2, 4 * NB), BF16),
            pltpu.SemaphoreType.DMA((nu,)),
            pltpu.SemaphoreType.DMA((2,)),
            pltpu.SemaphoreType.DMA((n_pieces, nt)),
            pltpu.SemaphoreType.DMA((n_pieces, nt)),
            pltpu.SemaphoreType.DMA((nt,)),
            pltpu.SemaphoreType.DMA((nt,)),
            pltpu.SemaphoreType.DMA((lf, ns)),
            pltpu.SemaphoreType.DMA((lf, ns)),
            pltpu.SemaphoreType.REGULAR,
        ],
        compiler_params=pltpu.CompilerParams(
            collective_id=0, has_side_effects=True, vmem_limit_bytes=50 * 2**20
        ),
    )(*(pltpu.with_memory_space_constraint(v, pltpu.HBM)
        for v in (series.transpose(1, 0, 2), freq_bins, weights.reshape(1, points))))
    cross, modes = pl.pallas_call(
        functools.partial(finish_kernel, nu),
        out_shape=(
            jax.ShapeDtypeStruct((lf, 2, NB, NB), F32),
            jax.ShapeDtypeStruct((lf, 2, 3, NB, points), BF16),
        ),
        in_specs=[vmem, vmem, vmem],
        out_specs=(hbm, hbm),
        scratch_shapes=[
            pltpu.VMEM((2, 3, NB, points), BF16),
            pltpu.SemaphoreType.DMA((lf - 1,)),
            pltpu.SemaphoreType.DMA,
            pltpu.SemaphoreType.DMA,
        ],
        compiler_params=pltpu.CompilerParams(vmem_limit_bytes=16 * 2**20),
    )(cross, early, x)
    return cross, modes.transpose(0, 1, 3, 2, 4)


def solution(mesh):
    nt, ns = mesh.shape["tm"], mesh.shape["pts"]
    in_specs = (P("tm", None, "pts"), P("pts"), P())
    out_specs = (P("tm", None, None, None), P("tm", None, None, None, "pts"))
    return jax.shard_map(
        functools.partial(on_device, nt, ns), mesh=mesh, in_specs=in_specs,
        out_specs=out_specs, check_vma=False
    )
```

```python
import functools

import jax
import jax.numpy as jnp
from jax import lax
from jax.experimental import pallas as pl
from jax.experimental.pallas import tpu as pltpu
from jax.sharding import PartitionSpec as P

NFFT = 512
NB = 32
NF = 16
ITERS = 4
HALF = NFFT // 2
UNIT = 256
MESH = pl.DeviceIdType.MESH
F32 = jnp.float32
BF16 = jnp.bfloat16


def half_wave(index):
    x = index.astype(F32) * F32(jnp.pi / 512.0)
    x2 = x * x
    c = F32(1.0 / 479001600.0)
    for v in (-1.0 / 3628800.0, 1.0 / 40320.0, -1.0 / 720.0, 1.0 / 24.0, -0.5, 1.0):
        c = c * x2 + F32(v)
    s = F32(-1.0 / 39916800.0)
    for v in (1.0 / 362880.0, -1.0 / 5040.0, 1.0 / 120.0, -1.0 / 6.0, 1.0):
        s = s * x2 + F32(v)
    return c, s * x


def build_table(freq_ref):
    shape = (2 * NF, HALF)
    row = lax.broadcasted_iota(jnp.int32, shape, 0)
    col = lax.broadcasted_iota(jnp.int32, shape, 1)
    freq = jnp.zeros(shape, jnp.int32)
    for f in range(NF):
        freq = jnp.where(row // 2 == f, freq_ref[f], freq)
    halves = []
    for h in range(2):
        n = col + h * HALF
        wc, _ = half_wave(n - HALF)
        window = wc * wc * F32((8.0 / (3.0 * NFFT)) ** 0.5)
        index = ((freq * n) & (NFFT - 1)) - HALF
        c, s = half_wave(index)
        cosine = 2.0 * s * s - 1.0
        minus_sine = 2.0 * s * c
        halves.append(jnp.where(row % 2 == 0, cosine, minus_sine) * window)
    return jnp.concatenate(halves, axis=0).astype(BF16)


def dot(left, right):
    return jnp.dot(left, right, preferred_element_type=F32)


def dot_t(left, right):
    return lax.dot_general(
        left, right, (((1,), (1,)), ((), ())), preferred_element_type=F32
    )


def split(value):
    hi = value.astype(BF16)
    return hi, (value - hi.astype(F32)).astype(BF16)


def dot_split(left, right):
    return dot(left[0], right[0]) + (dot(left[0], right[1]) + dot(left[1], right[0]))


def eye(size):
    row = lax.broadcasted_iota(jnp.int32, (size, size), 0)
    col = lax.broadcasted_iota(jnp.int32, (size, size), 1)
    return (row == col).astype(F32)


def normalized(real, imag):
    norm = jnp.sqrt(jnp.sum(real * real + imag * imag, axis=(0, 1), keepdims=True))
    upper = jnp.concatenate([real, -imag], axis=1)
    lower = jnp.concatenate([imag, real], axis=1)
    return jnp.concatenate([upper, lower], axis=0) * (1.0 / norm)


def inverse_roots(ys):
    half_three = 1.5 * eye(2 * NB)
    zs = None
    for it in range(ITERS):
        if zs is None:
            steps = [half_three - 0.5 * y for y in ys]
            ys = [dot_split(split(y), split(s)) for y, s in zip(ys, steps)]
            zs = steps
            continue
        zsp = [split(z) for z in zs]
        ysp = [split(y) for y in ys]
        steps = [half_three - 0.5 * dot_split(z, y) for z, y in zip(zsp, ysp)]
        ssp = [split(s) for s in steps]
        if it < ITERS - 1:
            ys = [dot_split(y, s) for y, s in zip(ysp, ssp)]
        zs = [dot_split(s, z) for s, z in zip(ssp, zsp)]
    return zs


def mix(root, rows_of, out, nu):
    for u in range(nu):
        y = dot(root, rows_of(u)).astype(BF16)
        cols = pl.ds(u // 3 * UNIT, UNIT)
        for i in range(2):
            out[i, u % 3, :, cols] = y[i * NB:(i + 1) * NB]


def finish_kernel(nu, cross_in, early, x, cross_ref, modes_ref,
                  out, early_sem, out_sem, cross_sem):
    lf = cross_in.shape[0]
    copies = [pltpu.make_async_copy(cross_in, cross_ref, cross_sem)]
    copies.append(
        pltpu.make_async_copy(early, modes_ref.at[pl.ds(0, lf - 1)], early_sem))
    for c in copies:
        c.start()
    y = normalized(cross_in[lf - 1, 0], cross_in[lf - 1, 1])
    (root,) = inverse_roots([y])
    mix(root.astype(BF16), lambda u: x[:, u * UNIT:(u + 1) * UNIT], out, nu)
    copies.append(pltpu.make_async_copy(out, modes_ref.at[lf - 1], out_sem))
    copies[-1].start()
    for c in copies:
        c.wait()


def kernel(nt, ns, lf, series, freq, weights, cross_ref, early_ref, x_ref,
           xbuf, table, wbuf, fbuf, mid, edge, send, land, esend, eland, xall,
           ar, in_sem, small_sem, send_sem, a_recv, e_recv, g_recv, go_sem):
    t = lax.axis_index("tm")
    s = lax.axis_index("pts")
    points = xbuf.shape[2]
    nq = points // UNIT
    nu = 3 * nq
    lanes = nu * UNIT
    lb = NB // nt
    per = 2 * lf
    rows = 2 * lb

    loads = [(u, 1) for u in range(3)] + [(u, 3) for u in range(3, nu, 3)]

    def series_copy(i):
        u, n = loads[i]
        at = (pl.ds(u % 3, n), slice(None), pl.ds(u // 3 * UNIT, UNIT))
        return pltpu.make_async_copy(series.at[at], xbuf.at[at], in_sem.at[i])

    freq_copy = pltpu.make_async_copy(freq, fbuf, small_sem.at[0])
    weight_copy = pltpu.make_async_copy(weights, wbuf, small_sem.at[1])
    freq_copy.start()
    for u in range(3):
        series_copy(u).start()
    barrier = pltpu.get_barrier_semaphore()
    for k in range(1, nt):
        pl.semaphore_signal(barrier, inc=1, device_id={"tm": lax.rem(t + k, nt)},
                            device_id_type=MESH)
    root = ns // 2

    @pl.when(s != root)
    def _():
        pl.semaphore_signal(barrier, inc=1, device_id={"pts": root}, device_id_type=MESH)

    for i in range(3, len(loads)):
        series_copy(i).start()
    weight_copy.start()
    freq_copy.wait()
    table[...] = build_table(fbuf)

    early = lf // 2
    pieces = [(0, early, u, 1) for u in range(3)]
    pieces += [(0, early, u, 3) for u in range(3, nu, 3)]
    for f in range(early, lf):
        if f < lf - 1:
            pieces.append((f, 1, 0, nu))
        else:
            pieces += [(f, 1, 0, nu - nu // 4), (f, 1, nu - nu // 4, nu // 4)]

    n_early = nu // 3 + 2
    pts_peer = {"pts": lax.rem(s + 1, ns)}
    tm_peer = {"tm": lax.rem(t + 1, nt)}

    def group(source, target, at, send_at, recv, peer):
        return pltpu.make_async_remote_copy(
            src_ref=source.at[at], dst_ref=target.at[at], send_sem=send_sem.at[send_at],
            recv_sem=recv, device_id=peer, device_id_type=MESH,
        )

    def stage(r):
        f, nf, u, n = pieces[n_early - 1 + r]
        if r == 0:
            u, n = 0, nu
        at = (pl.ds(1, nt - 1), pl.ds(f * rows, nf * rows), pl.ds(u * UNIT, n * UNIT))
        return group(land, land, at, 0, a_recv.at[r], tm_peer)

    def piece_copy(p, k):
        f, nf, u, n = pieces[p]
        to = lax.rem(t + k, nt)
        at = (pl.ds(f * rows, nf * rows), pl.ds(u * UNIT, n * UNIT))
        return pltpu.make_async_remote_copy(
            src_ref=send.at[(to, *at)], dst_ref=land.at[(k, *at)],
            send_sem=send_sem.at[0], recv_sem=a_recv.at[max(0, p - n_early + 1)],
            device_id={"tm": to}, device_id_type=MESH,
        )

    def edge_copy(k):
        to = lax.rem(t + k, nt)
        return pltpu.make_async_remote_copy(
            src_ref=esend.at[to], dst_ref=eland.at[k],
            send_sem=send_sem.at[1], recv_sem=e_recv,
            device_id={"tm": to}, device_id_type=MESH,
        )

    def gram_copy(f, k):
        return pltpu.make_async_remote_copy(
            src_ref=ar.at[f, 0], dst_ref=ar.at[f, k],
            send_sem=send_sem.at[2], recv_sem=g_recv.at[f],
            device_id={"pts": lax.rem(s + k, ns)}, device_id_type=MESH,
        )

    def rows_of(f):
        return xall.at[f] if f < lf - 1 else x_ref

    def transform(u):
        for i, (first_unit, _) in enumerate(loads):
            if first_unit == u:
                series_copy(i).wait()
        cols = pl.ds(u // 3 * UNIT, UNIT)
        at = pl.ds(u * UNIT, UNIT)
        first = None
        for j in range(lb):
            both = dot(table[...], xbuf[u % 3, j * HALF:(j + 1) * HALF, cols])
            if j == 0:
                edge[:, at] = both[2 * NF:]
            else:
                value = first + both[2 * NF:]
                for v in range(UNIT // 128):
                    mid[v, pl.ds(j - 1, 2 * NF, stride=lb), :] = value[:, v * 128:(v + 1) * 128]
            first = both[:2 * NF]
        for v in range(UNIT // 128):
            mid[v, pl.ds(lb - 1, 2 * NF, stride=lb), :] = first[:, v * 128:(v + 1) * 128]
        for d in range(nt):
            for v in range(UNIT // 128):
                send[d, :, pl.ds(u * UNIT + v * 128, 128)] = mid[
                    v, d * lf * rows:(d + 1) * lf * rows, :].astype(BF16)
        land[0, :, at] = send[t, :, at]

    p = 0
    for u in range(nu):
        transform(u)
        if u == 0:
            pl.semaphore_wait(barrier, nt - 1 + jnp.where(s == root, ns - 1, 0))

            @pl.when(s == root)
            def _():
                for k in range(1, ns):
                    pl.semaphore_signal(go_sem, inc=1, device_id={"pts": lax.rem(s + k, ns)},
                                        device_id_type=MESH)
        if pieces[p][2] + pieces[p][3] == u + 1:
            for k in range(1, nt):
                piece_copy(p, k).start()
            p += 1
    for d in range(nt):
        e = edge[d * per:(d + 1) * per, :]
        esend[d] = jnp.concatenate([e[:, :lanes // 2], e[:, lanes // 2:]], axis=0).astype(BF16)
    for k in range(1, nt):
        edge_copy(k).start()
    def begin(r):
        for k in range(1, nt):
            piece_copy(r, k).start()

    begin(p)
    eland[0] = esend[t]
    weight_copy.wait()

    last_row = lax.broadcasted_iota(jnp.int32, (lb, UNIT), 0) == lb - 1

    def unit_rows(f, u):
        at = pl.ds(u * UNIT, UNIT)
        half = u * UNIT // (lanes // 2)
        eat = pl.ds(u * UNIT - half * (lanes // 2), UNIT)
        parts = [[], []]
        for src in range(nt):
            x = land[lax.rem(t - src + nt, nt), f * rows:(f + 1) * rows, at].astype(F32)
            e = eland[lax.rem(t - src - 1 + nt, nt), :, eat].astype(F32)
            for i in range(2):
                r = half * per + 2 * f + i
                tail = jnp.where(last_row, e[r:r + 1], 0.0)
                parts[i].append(x[i * lb:(i + 1) * lb] + tail)
        return jnp.concatenate(parts[0] + parts[1], axis=0).astype(BF16)

    def gram(f, units, total):
        for u in units:
            x = unit_rows(f, u)
            rows_of(f)[:, u * UNIT:(u + 1) * UNIT] = x
            w = wbuf[:, u // 3 * UNIT:(u // 3 + 1) * UNIT]
            xw = (x.astype(F32) * w).astype(BF16)
            part = dot_t(xw, x)
            total = part if total is None else total + part
        return total

    def share(f, pair):
        real = pair[:NB, :NB] + pair[NB:, NB:]
        imag = pair[:NB, NB:] - pair[NB:, :NB]
        h = NB // 2
        packed = jnp.concatenate([real[:h], imag[:h], real[h:], imag[h:]], axis=1)
        ar[f, 0] = packed.astype(BF16)
        for k in range(1, ns):
            gram_copy(f, k).start()

    def collect(f):
        at = (f, pl.ds(1, ns - 1))
        group(ar, ar, at, 2, g_recv.at[f], pts_peer).wait_recv()
        total = None
        for src in range(ns):
            v = ar[f, lax.rem(s - src + ns, ns)].astype(F32)
            total = v if total is None else total + v
        real = jnp.concatenate([total[:, :NB], total[:, 2 * NB:3 * NB]], axis=0)
        imag = jnp.concatenate([total[:, NB:2 * NB], total[:, 3 * NB:]], axis=0)
        cross_ref[f, 0] = real
        cross_ref[f, 1] = imag
        return real, imag

    def finish(bins):
        roots = inverse_roots([normalized(*collect(f)) for f in bins])
        for f, root in zip(bins, roots):
            mix(root.astype(BF16), lambda u: xall[f, :, u * UNIT:(u + 1) * UNIT],
                early_ref.at[f], nu)

    def arrived(p):
        stage(p - n_early + 1).wait_recv()

    edges = group(eland, eland, pl.ds(1, nt - 1), 1, e_recv, tm_peer)
    edges.wait_recv()
    stage(0).wait_recv()
    grams = [gram(f, range(nu), None) for f in range(early)]

    @pl.when(s != root)
    def _():
        pl.semaphore_wait(go_sem, 1)

    for f in range(early):
        share(f, grams[f])
    begin(p + 1)
    for f in range(early, lf - 1):
        arrived(p)
        p += 1
        share(f, gram(f, range(nu), None))
        if f < lf - 2:
            begin(p + 1)
    for r in range(p + 1, len(pieces)):
        begin(r)
    finish(range(early))
    total = None
    for r in range(p, len(pieces)):
        arrived(r)
        _, _, u, n = pieces[r]
        total = gram(lf - 1, range(u, u + n), total)
    share(lf - 1, total)
    finish(range(early, lf - 1))
    collect(lf - 1)

    group(send, send, pl.ds(0, nt - 1), 0, a_recv.at[0], tm_peer).wait_send()
    edges.wait_send()
    group(ar, ar, (slice(None), pl.ds(1, ns - 1)), 2, g_recv.at[0], pts_peer).wait_send()


def on_device(nt, ns, series, weights, freq_bins):
    points = series.shape[2]
    nu = 3 * (points // UNIT)
    lanes = 3 * points
    lb, lf = NB // nt, NF // nt
    rows = 2 * lb
    hbm = pl.BlockSpec(memory_space=pl.ANY)
    vmem = pl.BlockSpec(memory_space=pltpu.VMEM)
    cross, early, x = pl.pallas_call(
        functools.partial(kernel, nt, ns, lf),
        out_shape=(
            jax.ShapeDtypeStruct((lf, 2, NB, NB), F32),
            jax.ShapeDtypeStruct((lf - 1, 2, 3, NB, points), BF16),
            jax.ShapeDtypeStruct((2 * NB, lanes), BF16),
        ),
        in_specs=[hbm, hbm, hbm],
        out_specs=(vmem, vmem, vmem),
        scratch_shapes=[
            pltpu.VMEM((3, series.shape[0], points), BF16),
            pltpu.VMEM((4 * NF, HALF), BF16),
            pltpu.VMEM((1, points), F32),
            pltpu.SMEM((NF,), jnp.int32),
            pltpu.VMEM((UNIT // 128, 2 * NF * lb, 128), F32),
            pltpu.VMEM((2 * NF, lanes), F32),
            pltpu.VMEM((nt, lf * rows, lanes), BF16),
            pltpu.VMEM((nt, lf * rows, lanes), BF16),
            pltpu.VMEM((nt, 4 * lf, lanes // 2), BF16),
            pltpu.VMEM((nt, 4 * lf, lanes // 2), BF16),
            pltpu.VMEM((lf - 1, 2 * NB, lanes), BF16),
            pltpu.VMEM((lf, ns, NB // 2, 4 * NB), BF16),
            pltpu.SemaphoreType.DMA((nu // 3 + 2,)),
            pltpu.SemaphoreType.DMA((2,)),
            pltpu.SemaphoreType.DMA((3,)),
            pltpu.SemaphoreType.DMA((lf - lf // 2 + 2,)),
            pltpu.SemaphoreType.DMA,
            pltpu.SemaphoreType.DMA((lf,)),
            pltpu.SemaphoreType.REGULAR,
        ],
        compiler_params=pltpu.CompilerParams(
            collective_id=0, has_side_effects=True, vmem_limit_bytes=50 * 2**20
        ),
    )(*(pltpu.with_memory_space_constraint(v, pltpu.HBM)
        for v in (series.transpose(1, 0, 2), freq_bins, weights.reshape(1, points))))
    cross, modes = pl.pallas_call(
        functools.partial(finish_kernel, nu),
        out_shape=(
            jax.ShapeDtypeStruct((lf, 2, NB, NB), F32),
            jax.ShapeDtypeStruct((lf, 2, 3, NB, points), BF16),
        ),
        in_specs=[vmem, vmem, vmem],
        out_specs=(hbm, hbm),
        scratch_shapes=[
            pltpu.VMEM((2, 3, NB, points), BF16),
            pltpu.SemaphoreType.DMA,
            pltpu.SemaphoreType.DMA,
            pltpu.SemaphoreType.DMA,
        ],
        compiler_params=pltpu.CompilerParams(vmem_limit_bytes=16 * 2**20),
    )(cross, early, x)
    return cross, modes.transpose(0, 1, 3, 2, 4)


def solution(mesh):
    nt, ns = mesh.shape["tm"], mesh.shape["pts"]
    in_specs = (P("tm", None, "pts"), P("pts"), P())
    out_specs = (P("tm", None, None, None), P("tm", None, None, None, "pts"))
    return jax.shard_map(
        functools.partial(on_device, nt, ns), mesh=mesh, in_specs=in_specs,
        out_specs=out_specs, check_vma=False
    )
```

```python
import functools

import jax
import jax.numpy as jnp
from jax import lax
from jax.experimental import pallas as pl
from jax.experimental.pallas import tpu as pltpu
from jax.sharding import PartitionSpec as P

NFFT = 512
NB = 32
NF = 16
HALF = NFFT // 2
UNIT = 256
MESH = pl.DeviceIdType.MESH
F32 = jnp.float32
BF16 = jnp.bfloat16


def half_wave(index):
    x = index.astype(F32) * F32(jnp.pi / 512.0)
    x2 = x * x
    c = F32(1.0 / 479001600.0)
    for v in (-1.0 / 3628800.0, 1.0 / 40320.0, -1.0 / 720.0, 1.0 / 24.0, -0.5, 1.0):
        c = c * x2 + F32(v)
    s = F32(-1.0 / 39916800.0)
    for v in (1.0 / 362880.0, -1.0 / 5040.0, 1.0 / 120.0, -1.0 / 6.0, 1.0):
        s = s * x2 + F32(v)
    return c, s * x


def build_table(freq_ref):
    shape = (2 * NF, HALF)
    row = lax.broadcasted_iota(jnp.int32, shape, 0)
    col = lax.broadcasted_iota(jnp.int32, shape, 1)
    freq = jnp.zeros(shape, jnp.int32)
    for f in range(NF):
        freq = jnp.where(row // 2 == f, freq_ref[f], freq)
    halves = []
    for h in range(2):
        n = col + h * HALF
        wc, _ = half_wave(n - HALF)
        window = wc * wc * F32((8.0 / (3.0 * NFFT)) ** 0.5)
        index = ((freq * n) & (NFFT - 1)) - HALF
        c, s = half_wave(index)
        cosine = 2.0 * s * s - 1.0
        minus_sine = 2.0 * s * c
        halves.append(jnp.where(row % 2 == 0, cosine, minus_sine) * window)
    return jnp.concatenate(halves, axis=0).astype(BF16)


def dot(left, right):
    return jnp.dot(left, right, preferred_element_type=F32)


def dot_t(left, right):
    return lax.dot_general(
        left, right, (((1,), (1,)), ((), ())), preferred_element_type=F32
    )


def split(value):
    hi = value.astype(BF16)
    return hi, (value - hi.astype(F32)).astype(BF16)


def dot_split(left, right):
    return dot(left[0], right[0]) + (dot(left[0], right[1]) + dot(left[1], right[0]))


def eye(size):
    row = lax.broadcasted_iota(jnp.int32, (size, size), 0)
    col = lax.broadcasted_iota(jnp.int32, (size, size), 1)
    return (row == col).astype(F32)


def normalized(real, imag):
    norm = jnp.sqrt(jnp.sum(real * real + imag * imag, axis=(0, 1), keepdims=True))
    upper = jnp.concatenate([real, -imag], axis=1)
    lower = jnp.concatenate([imag, real], axis=1)
    return jnp.concatenate([upper, lower], axis=0) * (1.0 / norm)


def inverse_root(e):
    s0 = 1.5 * eye(2 * NB) - 0.5 * e
    ep, s0p = split(e), split(s0)
    m1 = dot_split(split(dot_split(ep, s0p)), s0p)
    s1 = 1.5 * eye(2 * NB) - 0.5 * m1
    m1p, s1p = split(m1), split(s1)
    m1s = split(dot_split(m1p, s1p))
    z2 = dot_split(s0p, s1p)
    z2p = split(z2)
    s1s = split(dot_split(s1p, s1p))
    m2 = dot_split(m1s, s1p)
    m2p = split(m2)
    m1s2 = split(dot_split(m1s, m1s))
    z2s2 = split(dot_split(z2p, s1s))
    z2m = dot_split(z2p, m2p)
    z2mm = dot_split(z2s2, m1s2)
    mm = dot_split(m2p, m2p)
    high = dot_split(split(z2mm), split(0.0625 * mm - 0.5625 * m2))
    return (2.25 * z2 - 2.4375 * z2m + 1.6875 * z2mm) + high


def mix(root, rows_of, out, units):
    for u in units:
        y = dot(root, rows_of(u)).astype(BF16)
        cols = pl.ds(u // 3 * UNIT, UNIT)
        for i in range(2):
            out[i, u % 3, :, cols] = y[i * NB:(i + 1) * NB]


def finish_kernel(nu, cross_in, early, x, cross_ref, modes_ref,
                  out, early_sem, out_sem, cross_sem):
    lf = cross_in.shape[0]
    copies = [pltpu.make_async_copy(cross_in, cross_ref, cross_sem)]
    copies.append(
        pltpu.make_async_copy(early, modes_ref.at[pl.ds(0, lf - 1)], early_sem))
    for c in copies:
        c.start()
    y = normalized(cross_in[lf - 1, 0], cross_in[lf - 1, 1])
    root = inverse_root(y).astype(BF16)
    for h in range(2):
        mix(root, lambda u: x[:, u * UNIT:(u + 1) * UNIT], out,
            range(h * nu // 2, (h + 1) * nu // 2))
        at = (slice(None), slice(None), slice(None), pl.ds(h * nu // 6 * UNIT, nu // 6 * UNIT))
        copies.append(pltpu.make_async_copy(
            out.at[at], modes_ref.at[(lf - 1, *at)], out_sem.at[h]))
        copies[-1].start()
    for c in copies:
        c.wait()


def kernel(nt, ns, lf, series, freq, weights, cross_ref, early_ref, x_ref,
           xbuf, table, wbuf, fbuf, mid, edge, send, land, esend, eland, xall,
           ar, in_sem, small_sem, send_sem, a_recv, e_recv, g_recv, go_sem):
    t = lax.axis_index("tm")
    s = lax.axis_index("pts")
    points = xbuf.shape[2]
    nq = points // UNIT
    nu = 3 * nq
    lanes = nu * UNIT
    lb = NB // nt
    per = 2 * lf
    rows = 2 * lb

    loads = [(u, 1) for u in range(3)] + [(u, 3) for u in range(3, nu, 3)]

    def series_copy(i):
        u, n = loads[i]
        at = (pl.ds(u % 3, n), slice(None), pl.ds(u // 3 * UNIT, UNIT))
        return pltpu.make_async_copy(series.at[at], xbuf.at[at], in_sem.at[i])

    freq_copy = pltpu.make_async_copy(freq, fbuf, small_sem.at[0])
    weight_copy = pltpu.make_async_copy(weights, wbuf, small_sem.at[1])
    freq_copy.start()
    for u in range(3):
        series_copy(u).start()
    barrier = pltpu.get_barrier_semaphore()
    for k in range(1, nt):
        pl.semaphore_signal(barrier, inc=1, device_id={"tm": lax.rem(t + k, nt)},
                            device_id_type=MESH)
    root = ns // 2

    @pl.when(s != root)
    def _():
        pl.semaphore_signal(barrier, inc=1, device_id={"pts": root}, device_id_type=MESH)

    for i in range(3, len(loads)):
        series_copy(i).start()
    weight_copy.start()
    freq_copy.wait()
    table[...] = build_table(fbuf)

    early = lf // 2
    pieces = [(0, early, u, 1) for u in range(3)]
    pieces += [(0, early, u, 3) for u in range(3, nu, 3)]
    for f in range(early, lf):
        if f < lf - 1:
            pieces.append((f, 1, 0, nu))
        else:
            pieces += [(f, 1, 0, nu - nu // 4), (f, 1, nu - nu // 4, nu // 4)]

    n_early = nu // 3 + 2
    pts_peer = {"pts": lax.rem(s + 1, ns)}
    tm_peer = {"tm": lax.rem(t + 1, nt)}

    def group(source, target, at, send_at, recv, peer):
        return pltpu.make_async_remote_copy(
            src_ref=source.at[at], dst_ref=target.at[at], send_sem=send_sem.at[send_at],
            recv_sem=recv, device_id=peer, device_id_type=MESH,
        )

    def stage(r):
        f, nf, u, n = pieces[n_early - 1 + r]
        if r == 0:
            u, n = 0, nu
        at = (pl.ds(1, nt - 1), pl.ds(f * rows, nf * rows), pl.ds(u * UNIT, n * UNIT))
        return group(land, land, at, 0, a_recv.at[r], tm_peer)

    def piece_copy(p, k):
        f, nf, u, n = pieces[p]
        to = lax.rem(t + k, nt)
        at = (pl.ds(f * rows, nf * rows), pl.ds(u * UNIT, n * UNIT))
        return pltpu.make_async_remote_copy(
            src_ref=send.at[(to, *at)], dst_ref=land.at[(k, *at)],
            send_sem=send_sem.at[0], recv_sem=a_recv.at[max(0, p - n_early + 1)],
            device_id={"tm": to}, device_id_type=MESH,
        )

    def edge_copy(k):
        to = lax.rem(t + k, nt)
        return pltpu.make_async_remote_copy(
            src_ref=esend.at[to], dst_ref=eland.at[k],
            send_sem=send_sem.at[1], recv_sem=e_recv,
            device_id={"tm": to}, device_id_type=MESH,
        )

    def gram_copy(f, k):
        return pltpu.make_async_remote_copy(
            src_ref=ar.at[f, 0], dst_ref=ar.at[f, k],
            send_sem=send_sem.at[2], recv_sem=g_recv.at[f],
            device_id={"pts": lax.rem(s + k, ns)}, device_id_type=MESH,
        )

    def rows_of(f):
        return xall.at[f] if f < lf - 1 else x_ref

    def transform(u):
        for i, (first_unit, _) in enumerate(loads):
            if first_unit == u:
                series_copy(i).wait()
        cols = pl.ds(u // 3 * UNIT, UNIT)
        at = pl.ds(u * UNIT, UNIT)
        first = None
        for j in range(lb):
            both = dot(table[...], xbuf[u % 3, j * HALF:(j + 1) * HALF, cols])
            if j == 0:
                edge[:, at] = both[2 * NF:]
            else:
                value = first + both[2 * NF:]
                for v in range(UNIT // 128):
                    mid[v, pl.ds(j - 1, 2 * NF, stride=lb), :] = value[:, v * 128:(v + 1) * 128]
            first = both[:2 * NF]
        for v in range(UNIT // 128):
            mid[v, pl.ds(lb - 1, 2 * NF, stride=lb), :] = first[:, v * 128:(v + 1) * 128]
        for d in range(nt):
            for v in range(UNIT // 128):
                send[d, :, pl.ds(u * UNIT + v * 128, 128)] = mid[
                    v, d * lf * rows:(d + 1) * lf * rows, :].astype(BF16)
        land[0, :, at] = send[t, :, at]

    p = 0
    for u in range(nu):
        transform(u)
        if u == 0:
            pl.semaphore_wait(barrier, nt - 1 + jnp.where(s == root, ns - 1, 0))

            @pl.when(s == root)
            def _():
                for k in range(1, ns):
                    pl.semaphore_signal(go_sem, inc=1, device_id={"pts": lax.rem(s + k, ns)},
                                        device_id_type=MESH)
        if pieces[p][2] + pieces[p][3] == u + 1:
            for k in range(1, nt):
                piece_copy(p, k).start()
            p += 1
    for d in range(nt):
        e = edge[d * per:(d + 1) * per, :]
        esend[d] = jnp.concatenate([e[:, :lanes // 2], e[:, lanes // 2:]], axis=0).astype(BF16)
    for k in range(1, nt):
        edge_copy(k).start()
    def begin(r):
        for k in range(1, nt):
            piece_copy(r, k).start()

    begin(p)
    eland[0] = esend[t]
    weight_copy.wait()

    last_row = lax.broadcasted_iota(jnp.int32, (lb, UNIT), 0) == lb - 1

    def unit_rows(f, u):
        at = pl.ds(u * UNIT, UNIT)
        half = u * UNIT // (lanes // 2)
        eat = pl.ds(u * UNIT - half * (lanes // 2), UNIT)
        parts = [[], []]
        for src in range(nt):
            x = land[lax.rem(t - src + nt, nt), f * rows:(f + 1) * rows, at].astype(F32)
            e = eland[lax.rem(t - src - 1 + nt, nt), :, eat].astype(F32)
            for i in range(2):
                r = half * per + 2 * f + i
                tail = jnp.where(last_row, e[r:r + 1], 0.0)
                parts[i].append(x[i * lb:(i + 1) * lb] + tail)
        return jnp.concatenate(parts[0] + parts[1], axis=0).astype(BF16)

    def gram(f, units, total):
        for u in units:
            x = unit_rows(f, u)
            rows_of(f)[:, u * UNIT:(u + 1) * UNIT] = x
            w = wbuf[:, u // 3 * UNIT:(u // 3 + 1) * UNIT]
            xw = (x.astype(F32) * w).astype(BF16)
            part = dot_t(xw, x)
            total = part if total is None else total + part
        return total

    def share(f, pair):
        real = pair[:NB, :NB] + pair[NB:, NB:]
        imag = pair[:NB, NB:] - pair[NB:, :NB]
        h = NB // 2
        packed = jnp.concatenate([real[:h], imag[:h], real[h:], imag[h:]], axis=1)
        ar[f, 0] = packed.astype(BF16)
        for k in range(1, ns):
            gram_copy(f, k).start()

    def collect(f):
        at = (f, pl.ds(1, ns - 1))
        group(ar, ar, at, 2, g_recv.at[f], pts_peer).wait_recv()
        total = None
        for src in range(ns):
            v = ar[f, lax.rem(s - src + ns, ns)].astype(F32)
            total = v if total is None else total + v
        real = jnp.concatenate([total[:, :NB], total[:, 2 * NB:3 * NB]], axis=0)
        imag = jnp.concatenate([total[:, NB:2 * NB], total[:, 3 * NB:]], axis=0)
        cross_ref[f, 0] = real
        cross_ref[f, 1] = imag
        return real, imag

    def finish(bins):
        roots = [inverse_root(normalized(*collect(f))) for f in bins]
        for f, root in zip(bins, roots):
            mix(root.astype(BF16), lambda u: xall[f, :, u * UNIT:(u + 1) * UNIT],
                early_ref.at[f], range(nu))

    def arrived(p):
        stage(p - n_early + 1).wait_recv()

    edges = group(eland, eland, pl.ds(1, nt - 1), 1, e_recv, tm_peer)
    edges.wait_recv()
    stage(0).wait_recv()
    grams = [gram(f, range(nu), None) for f in range(early)]

    @pl.when(s != root)
    def _():
        pl.semaphore_wait(go_sem, 1)

    for f in range(early):
        share(f, grams[f])
    begin(p + 1)
    for f in range(early, lf - 1):
        arrived(p)
        p += 1
        share(f, gram(f, range(nu), None))
        if f < lf - 2:
            begin(p + 1)
    for r in range(p + 1, len(pieces)):
        begin(r)
    finish(range(early))
    total = None
    for r in range(p, len(pieces)):
        arrived(r)
        _, _, u, n = pieces[r]
        total = gram(lf - 1, range(u, u + n), total)
    share(lf - 1, total)
    finish(range(early, lf - 1))
    collect(lf - 1)

    group(send, send, pl.ds(0, nt - 1), 0, a_recv.at[0], tm_peer).wait_send()
    edges.wait_send()
    group(ar, ar, (slice(None), pl.ds(1, ns - 1)), 2, g_recv.at[0], pts_peer).wait_send()


def on_device(nt, ns, series, weights, freq_bins):
    points = series.shape[2]
    nu = 3 * (points // UNIT)
    lanes = 3 * points
    lb, lf = NB // nt, NF // nt
    rows = 2 * lb
    hbm = pl.BlockSpec(memory_space=pl.ANY)
    vmem = pl.BlockSpec(memory_space=pltpu.VMEM)
    cross, early, x = pl.pallas_call(
        functools.partial(kernel, nt, ns, lf),
        out_shape=(
            jax.ShapeDtypeStruct((lf, 2, NB, NB), F32),
            jax.ShapeDtypeStruct((lf - 1, 2, 3, NB, points), BF16),
            jax.ShapeDtypeStruct((2 * NB, lanes), BF16),
        ),
        in_specs=[hbm, hbm, hbm],
        out_specs=(vmem, vmem, vmem),
        scratch_shapes=[
            pltpu.VMEM((3, series.shape[0], points), BF16),
            pltpu.VMEM((4 * NF, HALF), BF16),
            pltpu.VMEM((1, points), F32),
            pltpu.SMEM((NF,), jnp.int32),
            pltpu.VMEM((UNIT // 128, 2 * NF * lb, 128), F32),
            pltpu.VMEM((2 * NF, lanes), F32),
            pltpu.VMEM((nt, lf * rows, lanes), BF16),
            pltpu.VMEM((nt, lf * rows, lanes), BF16),
            pltpu.VMEM((nt, 4 * lf, lanes // 2), BF16),
            pltpu.VMEM((nt, 4 * lf, lanes // 2), BF16),
            pltpu.VMEM((lf - 1, 2 * NB, lanes), BF16),
            pltpu.VMEM((lf, ns, NB // 2, 4 * NB), BF16),
            pltpu.SemaphoreType.DMA((nu // 3 + 2,)),
            pltpu.SemaphoreType.DMA((2,)),
            pltpu.SemaphoreType.DMA((3,)),
            pltpu.SemaphoreType.DMA((lf - lf // 2 + 2,)),
            pltpu.SemaphoreType.DMA,
            pltpu.SemaphoreType.DMA((lf,)),
            pltpu.SemaphoreType.REGULAR,
        ],
        compiler_params=pltpu.CompilerParams(
            collective_id=0, has_side_effects=True, vmem_limit_bytes=50 * 2**20
        ),
    )(*(pltpu.with_memory_space_constraint(v, pltpu.HBM)
        for v in (series.transpose(1, 0, 2), freq_bins, weights.reshape(1, points))))
    cross, modes = pl.pallas_call(
        functools.partial(finish_kernel, nu),
        out_shape=(
            jax.ShapeDtypeStruct((lf, 2, NB, NB), F32),
            jax.ShapeDtypeStruct((lf, 2, 3, NB, points), BF16),
        ),
        in_specs=[vmem, vmem, vmem],
        out_specs=(hbm, hbm),
        scratch_shapes=[
            pltpu.VMEM((2, 3, NB, points), BF16),
            pltpu.SemaphoreType.DMA,
            pltpu.SemaphoreType.DMA((2,)),
            pltpu.SemaphoreType.DMA,
        ],
        compiler_params=pltpu.CompilerParams(vmem_limit_bytes=16 * 2**20),
    )(cross, early, x)
    return cross, modes.transpose(0, 1, 3, 2, 4)


def solution(mesh):
    nt, ns = mesh.shape["tm"], mesh.shape["pts"]
    in_specs = (P("tm", None, "pts"), P("pts"), P())
    out_specs = (P("tm", None, None, None), P("tm", None, None, None, "pts"))
    return jax.shard_map(
        functools.partial(on_device, nt, ns), mesh=mesh, in_specs=in_specs,
        out_specs=out_specs, check_vma=False
    )
```
